32 devices in a mesh: sample: 2 (over x), stretch: 4 (over z), band: 4 (over y, core).
Axes of the slice: x: 2, y: 2, z: 4, core: 2. Of those that a mesh axis runs over, the one named last changes fastest.
Arguments:
- latents: bfloat16 [32, 8, 16, 128], P('sample', 'stretch', 'band'), may hold values from -6 to 6
- lengths: int32 [32], replicated, may hold values from 1 to 8, as said below
- dest_slot: int32 [32], replicated, may hold values from 0 to 31, as said below
- w_in: bfloat16 [432, 384], replicated, may hold values from -0.3125 to 0.3125
- b_in: float32 [384], replicated, may hold values from -3 to 3
- gain_mid: float32 [384], replicated, may hold values from 0.25 to 1.75
- w_mid: bfloat16 [10368, 384], replicated, may hold values from -0.0625 to 0.0625
- b_mid: float32 [384], replicated, may hold values from -3 to 3
- w_proj: bfloat16 [384, 1536], replicated, may hold values from -0.3125 to 0.3125
- gain_tok: float32 [1536], replicated, may hold values from 0.25 to 1.75
- w_gate: bfloat16 [1536, 8960], P('sample', ('stretch', 'band')), may hold values from -0.15625 to 0.15625
- w_up: bfloat16 [1536, 8960], P('sample', ('stretch', 'band')), may hold values from -0.15625 to 0.15625
- w_down: bfloat16 [8960, 1536], P(('stretch', 'band'), 'sample'), may hold values from -0.0625 to 0.0625
- w_score: float32 [1536], replicated, may hold values from -0.15625 to 0.15625
Outputs:
- decoded: bfloat16 [32, 8, 16, 3072], P('sample', 'stretch', 'band')
- scores: float32 [32], replicated
The draws below stay inside these ranges and needn't reach their ends.
Inputs may be any that keep to these rules, and one draw needn't show every extreme that they name: `lengths`: every clip has 1 or more frames; some clip has 8. `dest_slot`: a permutation; slot k belongs to decoder group k // 16; diffusion group g (clips g * 16 onward) sends exactly 8 clips to every decoder group, into that group's slots g * 8 to g * 8 + 7.
All inputs are finite; a program needn't handle non-finite values.
Results may differ from the reference program's by a relative error of at most 0.0085.
Values may be sent and summed in bfloat16 or wider, within the bound.
No kernel may reach another device: no remote copies, remote signals or barrier semaphores. Data moves between devices by JAX's collectives and lax.ppermute only.
A program may use at most 128 MiB of HBM per device.

```python
import jax
import jax.numpy as jnp
from jax import lax

LC = 16
CH = 384
DR = 1536
FF = 8960
CLIP_DEV = 16
W = 8
F = 8
H = 16
C = 32
SENDS = 8
N_SAMPLE = 2


def clip_lengths(key):
    base_len = jax.random.randint(jax.random.fold_in(key, 11), (C,), 1, F + 1)
    longest = jax.random.randint(jax.random.fold_in(key, 12), (), 0, C)
    return jnp.where(jnp.arange(C) == longest, F, base_len).astype(jnp.int32)


def draw_lengths(key, part):
    return clip_lengths(key)


def draw_dest_slot(key, part):
    clip_len = clip_lengths(key)
    breaker = jax.random.permutation(jax.random.fold_in(key, 13), C).astype(jnp.int32)
    ranking = (clip_len * C + breaker).reshape(N_SAMPLE, CLIP_DEV)
    rank_pos = jnp.argsort(jnp.argsort(ranking, axis=1), axis=1).astype(jnp.int32)
    decoder = rank_pos % N_SAMPLE
    within = rank_pos // N_SAMPLE
    source = jnp.arange(N_SAMPLE, dtype=jnp.int32)[:, None]
    slot_ids = decoder * CLIP_DEV + source * SENDS + within
    return slot_ids.reshape(C).astype(jnp.int32)


def draw_latents(key, part):
    noise_key = jax.random.fold_in(key, 31)
    offset_key = jax.random.fold_in(key, 32)
    noise = jax.random.normal(noise_key, (C, F, H, W, LC), jnp.float32)
    offset = 1.5 * jax.random.normal(offset_key, (C, F, 1, 1, LC), jnp.float32)
    values = jnp.clip(noise + offset, -6.0, 6.0)
    return values.reshape(C, F, H, W * LC).astype(jnp.bfloat16)


def shard_levels(key, dims, pieces, least, top_value):
    level, own = 1.0, jax.random.fold_in(key, 6)
    for axis_at, blocks in pieces:
        draws = jnp.exp(jax.random.uniform(jax.random.fold_in(own, axis_at), (blocks,), jnp.float32, least / len(pieces), top_value / len(pieces)))
        level = level * jnp.repeat(draws, dims[axis_at] // blocks).reshape([-1 if axis == axis_at else 1 for axis in range(len(dims))])
    return level


def gaussian(key, extent, width, limit, pieces=(), kind=jnp.bfloat16):
    drawn = jax.random.normal(key, extent, jnp.float32) * width
    if len(pieces) > 0:
        drawn = shard_levels(key, extent, pieces, -0.22, 0.18) * drawn
    return jnp.clip(drawn, min=-limit, max=limit).astype(kind)


def setup_inputs(seed: int = 0) -> dict:
    key_of = jax.random.split(jax.random.key(seed), 15)
    return {
        "latents": draw_latents(jax.random.fold_in(key_of[14], 71), 0),
        "lengths": draw_lengths(jax.random.fold_in(key_of[14], 71), 0),
        "dest_slot": draw_dest_slot(jax.random.fold_in(key_of[14], 71), 0),
        "w_in": gaussian(key_of[3], (27 * LC, CH), (27 * LC) ** -0.5, 0.3125),
        "b_in": gaussian(key_of[4], (CH,), 0.5, 3.0, (), jnp.float32),
        "gain_mid": jnp.clip(1.0 + 0.15 * jax.random.normal(key_of[5], (CH,), jnp.float32), 0.25, 1.75),
        "w_mid": gaussian(key_of[6], (27 * CH, CH), (27 * CH) ** -0.5, 0.0625),
        "b_mid": gaussian(key_of[7], (CH,), 0.5, 3.0, (), jnp.float32),
        "w_proj": gaussian(key_of[8], (CH, DR), CH ** -0.5, 0.3125),
        "gain_tok": jnp.clip(1.0 + 0.15 * jax.random.normal(key_of[9], (DR,), jnp.float32), 0.25, 1.75),
        "w_gate": gaussian(key_of[10], (DR, FF), DR ** -0.5, 0.15625, ((0, 2), (1, 16))),
        "w_up": gaussian(key_of[11], (DR, FF), DR ** -0.5, 0.15625, ((0, 2), (1, 16))),
        "w_down": gaussian(key_of[12], (FF, DR), FF ** -0.5, 0.0625, ((0, 16), (1, 2))),
        "w_score": gaussian(key_of[13], (DR,), DR ** -0.5, 0.15625, (), jnp.float32),
    }


def conv_taps(extended, weight, frames_out, rows_out, cols_out):
    clip_total = extended.shape[0]
    chans_in = extended.shape[-1]
    running_sum = jnp.zeros((clip_total * frames_out * rows_out * cols_out, weight.shape[1]), jnp.float32)
    for tap_index in range(27):
        shift_t, remain = divmod(tap_index, 9)
        shift_r, shift_c = divmod(remain, 3)
        window = extended[:, shift_t:shift_t + frames_out, shift_r:shift_r + rows_out, shift_c:shift_c + cols_out, :]
        window = window.reshape(-1, chans_in)
        running_sum = running_sum + jnp.dot(window, weight[tap_index * chans_in:(tap_index + 1) * chans_in], preferred_element_type=jnp.float32)
    return running_sum.reshape(clip_total, frames_out, rows_out, cols_out, -1)

def activate(first_out, gain_mid):
    values = first_out.astype(jnp.float32)
    scaled = values * lax.rsqrt(lax.optimization_barrier(jnp.mean(values * values, axis=-1, keepdims=True)) + 1e-06) * gain_mid
    return jax.nn.silu(scaled).astype(jnp.bfloat16)

def reference(latents, lengths, dest_slot, w_in, b_in, gain_mid, w_mid, b_mid, w_proj, gain_tok, w_gate, w_up, w_down, w_score):
    inverse = jnp.zeros((C,), jnp.int32).at[dest_slot].set(jnp.arange(C, dtype=jnp.int32))
    routed = latents[inverse]
    len_slot = lengths[inverse]
    valid_frames = jnp.arange(F, dtype=jnp.int32)[None, :] < len_slot[:, None]
    cells = routed.reshape(C, F, H, W, LC)
    cells = jnp.where(valid_frames[:, :, None, None, None], cells, jnp.zeros((), jnp.bfloat16))

    def decode_clip(packed):
        clip_cells, clip_valid = packed
        extended = jnp.pad(clip_cells, ((2, 0), (1, 1), (1, 1), (0, 0)))[None]
        first_out = (conv_taps(extended, w_in, F, H, W) + b_in).astype(jnp.bfloat16)
        hidden_in = activate(first_out, gain_mid)
        second_in = jnp.pad(hidden_in[0], ((2, 0), (1, 1), (1, 1), (0, 0)))[None]
        mixed_out = first_out.astype(jnp.float32) + conv_taps(second_in, w_mid, F, H, W) + b_mid
        mixed_out = jnp.where(clip_valid[None, :, None, None, None], mixed_out, 0.0).astype(jnp.bfloat16)[0]
        pooled = lax.optimization_barrier(jnp.mean(mixed_out.astype(jnp.float32), axis=(1, 2)))
        return (mixed_out, pooled)
    decoded, pooled = lax.map(decode_clip, (cells, valid_frames))
    tokens = jnp.dot(pooled.astype(jnp.bfloat16).reshape(C * F, CH), w_proj, preferred_element_type=jnp.float32).astype(jnp.bfloat16)
    token_f = tokens.astype(jnp.float32)
    normed = (token_f * lax.rsqrt(lax.optimization_barrier(jnp.mean(token_f * token_f, axis=-1, keepdims=True)) + 1e-06) * gain_tok).astype(jnp.bfloat16)
    gate_sum = jnp.dot(normed, w_gate, preferred_element_type=jnp.float32)
    up_sum = jnp.dot(normed, w_up, preferred_element_type=jnp.float32)
    hidden = (jax.nn.silu(gate_sum) * up_sum).astype(jnp.bfloat16)
    down = jnp.dot(hidden, w_down, preferred_element_type=jnp.float32)
    tok_score = lax.optimization_barrier(jnp.sum((token_f + down) * w_score, axis=-1)).reshape(C, F)
    slot_score = lax.optimization_barrier(jnp.sum(jnp.where(valid_frames, tok_score, 0.0), axis=1)) / len_slot.astype(jnp.float32)
    scores = slot_score[dest_slot]
    return (decoded.reshape(C, F, H, W * CH), scores)
```

```python
import functools

import jax
import jax.numpy as jnp
from jax import lax
from jax.experimental import pallas as pl
from jax.experimental.pallas import tpu as pltpu
from jax.sharding import PartitionSpec as P

ALL = ("sample", "stretch", "band")
TAPS = 3
BEHIND = 2 * (TAPS - 1)


def decode_kernel(
    edge_ref,
    len_ref,
    *refs,
    blocks,
    frames,
    rows,
    widths,
    clips,
    chans,
):
    lat_refs = refs[:blocks]
    (w_in_ref, b_in_ref, gain_ref, w_mid_hbm, b_mid_ref, out_ref, pool_ref) = refs[
        blocks : blocks + 7
    ]
    x1_ref, wt_ref, act_ref, first_ref, acc_ref, wm_ref, sem = refs[blocks + 7 :]
    chans_lat = w_in_ref.shape[0] // 27
    lanes = widths * chans_lat
    frames_act = frames + TAPS - 1
    rows_act = rows + TAPS - 1
    per_frame = rows_act * clips
    weights_copy = pltpu.make_async_copy(w_mid_hbm, wm_ref, sem)
    weights_copy.start()

    skip = blocks * frames - (frames_act + TAPS - 1)

    def frame(index):
        return lat_refs[(index + skip) // frames], (index + skip) % frames

    for j in range(9):
        dt, dr = divmod(j, 3)
        for f in range(frames_act):
            ref, at = frame(f + dt)
            x1_ref[f * per_frame : (f + 1) * per_frame, j * lanes : (j + 1) * lanes] = ref[
                at, dr : dr + rows_act
            ].reshape(per_frame, lanes)
    wt_ref[...] = jnp.zeros_like(wt_ref)
    act_ref[:, :, 0] = jnp.zeros((frames_act, rows_act, clips, chans), jnp.bfloat16)
    act_ref[:, :, widths + 1] = jnp.zeros((frames_act, rows_act, clips, chans), jnp.bfloat16)

    def column(q, carry):
        here = pl.multiple_of(q * chans_lat, chans_lat)
        before = pl.multiple_of(jnp.maximum(q - 1, 0) * chans_lat, chans_lat)
        for j in range(9):
            wt_ref[j, pl.ds(before, chans_lat), :] = jnp.zeros((chans_lat, chans), jnp.bfloat16)
            wt_ref[j, pl.ds(here, 3 * chans_lat), :] = w_in_ref[
                j * 3 * chans_lat : (j + 1) * 3 * chans_lat, :
            ]
        weight = wt_ref[:, chans_lat : chans_lat + lanes, :].reshape(9 * lanes, chans)
        total = jnp.dot(x1_ref[...], weight, preferred_element_type=jnp.float32)
        first = (total + b_in_ref[...]).astype(jnp.bfloat16)
        values = first.astype(jnp.float32)
        square = jnp.sum(values * values, axis=-1, keepdims=True) * (1.0 / chans)
        scaled = values * lax.rsqrt(square + 1e-06) * gain_ref[...]
        half = 0.5 * scaled
        act = (half + half * jnp.tanh(half)).astype(jnp.bfloat16)
        act_ref[:, :, q + 1] = act.reshape(frames_act, rows_act, clips, chans)
        first_ref[:, :, q] = first.reshape(frames_act, rows_act, clips, chans)[
            TAPS - 1 :, 1 : 1 + rows
        ]
        return carry

    lax.fori_loop(0, widths, column, 0)

    @pl.when(edge_ref[0] == 1)
    def _():
        act_ref[:, 0] = jnp.zeros((frames_act, widths + 2, clips, chans), jnp.bfloat16)

    @pl.when(edge_ref[1] == 1)
    def _():
        act_ref[:, rows_act - 1] = jnp.zeros((frames_act, widths + 2, clips, chans), jnp.bfloat16)

    @pl.when(edge_ref[2] == 1)
    def _():
        act_ref[0 : TAPS - 1] = jnp.zeros(
            (TAPS - 1, rows_act, widths + 2, clips, chans), jnp.bfloat16
        )

    weights_copy.wait()
    cells = rows * widths * clips

    def window(t, tap):
        dt = tap // 9
        dr = (tap % 9) // 3
        dq = tap % 3
        return act_ref[t + dt, pl.ds(dr, rows), pl.ds(dq, widths)].reshape(cells, chans)

    for t in range(frames):
        acc_ref[...] = jnp.dot(
            window(t, 26), wm_ref[26 * chans : 27 * chans, :], preferred_element_type=jnp.float32
        )

        def pair(p, carry, t=t):
            both = jnp.concatenate([window(t, 2 * p), window(t, 2 * p + 1)], axis=-1)
            at = pl.multiple_of(p * 2 * chans, 2 * chans)
            acc_ref[...] += jnp.dot(
                both, wm_ref[pl.ds(at, 2 * chans), :], preferred_element_type=jnp.float32
            )
            return carry

        lax.fori_loop(0, 13, pair, 0)
        live = (edge_ref[3] + t) < len_ref[:, 0:1]
        pooled = jnp.zeros((clips, chans), jnp.float32)
        for r in range(rows):
            for q in range(widths):
                at = (r * widths + q) * clips
                mixed = (
                    first_ref[t, r, q].astype(jnp.float32)
                    + acc_ref[at : at + clips, :]
                    + b_mid_ref[...]
                )
                done = jnp.where(live, mixed, 0.0).astype(jnp.bfloat16)
                out_ref[t, r, :, q * chans : (q + 1) * chans] = done
                pooled = pooled + done.astype(jnp.float32)
        pool_ref[t] = pooled


def decode(edges, lens, blocks, w_in, b_in, gain_mid, w_mid, b_mid, frames, rows, widths):
    chans = w_in.shape[1]
    clips = blocks[0].shape[2]
    lanes = blocks[0].shape[3]
    chans_lat = lanes // widths
    frames_act = frames + TAPS - 1
    rows_act = rows + TAPS - 1
    vmem = pl.BlockSpec(memory_space=pltpu.VMEM)
    kernel = functools.partial(
        decode_kernel,
        blocks=len(blocks),
        frames=frames,
        rows=rows,
        widths=widths,
        clips=clips,
        chans=chans,
    )
    flops = 2 * frames * rows * widths * clips * chans * 27 * chans
    return pl.pallas_call(
        kernel,
        out_shape=(
            jax.ShapeDtypeStruct((frames, rows, clips, widths * chans), jnp.bfloat16),
            jax.ShapeDtypeStruct((frames, clips, chans), jnp.float32),
        ),
        in_specs=[pl.BlockSpec(memory_space=pltpu.SMEM), vmem]
        + [vmem] * len(blocks)
        + [vmem, vmem, vmem, pl.BlockSpec(memory_space=pl.ANY), vmem],
        out_specs=(vmem, vmem),
        scratch_shapes=[
            pltpu.VMEM((frames_act * rows_act * clips, 9 * lanes), jnp.bfloat16),
            pltpu.VMEM((9, lanes + 2 * chans_lat, chans), jnp.bfloat16),
            pltpu.VMEM((frames_act, rows_act, widths + 2, clips, chans), jnp.bfloat16),
            pltpu.VMEM((frames, rows, widths, clips, chans), jnp.bfloat16),
            pltpu.VMEM((rows * widths * clips, chans), jnp.float32),
            pltpu.VMEM(w_mid.shape, jnp.bfloat16),
            pltpu.SemaphoreType.DMA,
        ],
        compiler_params=pltpu.CompilerParams(vmem_limit_bytes=40 * 1024 * 1024),
        cost_estimate=pl.CostEstimate(
            flops=flops, bytes_accessed=w_mid.size * 2, transcendentals=0
        ),
    )(
        edges,
        lens,
        *blocks,
        w_in,
        b_in.reshape(1, -1),
        gain_mid.reshape(1, -1),
        w_mid,
        b_mid.reshape(1, -1),
    )


def spread(value, axes):
    count = 1
    for axis in axes:
        count *= lax.axis_size(axis)
    return lax.all_to_all(
        jnp.broadcast_to(value[None], (count,) + value.shape), axes, 0, 0, tiled=True
    )


def body(
    latents,
    lengths,
    dest_slot,
    w_in,
    b_in,
    gain_mid,
    w_mid,
    b_mid,
    w_proj,
    gain_tok,
    w_gate,
    w_up,
    w_down,
    w_score,
):
    clips, frames, rows, lanes = latents.shape
    n_sample, n_stretch, n_band = (lax.axis_size(axis) for axis in ALL)
    chans_lat = w_in.shape[0] // 27
    chans = w_in.shape[1]
    widths = lanes // chans_lat
    sends = clips // n_sample
    group = lax.axis_index("sample")
    stretch = lax.axis_index("stretch")
    band = lax.axis_index("band")
    all_clips = dest_slot.shape[0]
    frame0 = stretch * frames

    my_dest = lax.dynamic_slice_in_dim(dest_slot, group * clips, clips)
    my_len = lax.dynamic_slice_in_dim(lengths, group * clips, clips)
    target = jnp.arange(n_sample, dtype=jnp.int32)[:, None] * clips + group * sends
    target = (target + jnp.arange(sends, dtype=jnp.int32)[None, :]).reshape(-1)
    select = (target[:, None] == my_dest[None, :]).astype(jnp.bfloat16)
    frame_ids = frame0 + jnp.arange(frames, dtype=jnp.int32)
    live = frame_ids[None, :] < my_len[:, None]
    masked = jnp.where(live[:, :, None, None], latents, jnp.zeros((), jnp.bfloat16))
    routed = jnp.einsum(
        "kc,ctrl->trkl", select, masked, preferred_element_type=jnp.float32
    ).astype(jnp.bfloat16)
    routed = routed.reshape(frames, rows, n_sample, sends, lanes).transpose(2, 0, 1, 3, 4)
    outgoing = jnp.broadcast_to(
        routed[:, None], (n_sample, n_band, frames, rows, sends, lanes)
    ).reshape(n_sample * n_band, frames, rows, sends, lanes)
    got = lax.all_to_all(outgoing, ("sample", "band"), 0, 0, tiled=True)
    got = got.reshape(n_sample, n_band, frames, rows, sends, lanes)
    got = got.transpose(2, 1, 3, 0, 4, 5).reshape(frames, n_band * rows, clips, lanes)
    got = jnp.pad(got, ((0, 0), (2, 2), (0, 0), (0, 0)))
    own = lax.dynamic_slice_in_dim(got, band * rows, rows + 4, axis=1)
    hops = -(-BEHIND // frames)
    blocks = [
        lax.ppermute(own, "stretch", [(i, i + d) for i in range(n_stretch - d)])
        for d in range(hops, 0, -1)
    ] + [own]

    units = w_gate.shape[1] // n_sample

    def of_units(weight, index, axis):
        return lax.dynamic_slice_in_dim(weight, index * units, units, axis=axis)

    own_v = jnp.sum(
        w_down.astype(jnp.float32)
        * lax.dynamic_slice_in_dim(w_score, group * w_down.shape[1], w_down.shape[1])[None, :],
        axis=-1,
    )
    depth = w_gate.shape[0]
    gate_parts, up_parts, v_unit = [None], [None], of_units(own_v, group, 0)
    for d in range(1, n_sample):
        route = [(i, (i + d) % n_sample) for i in range(n_sample)]
        other = (group + d) % n_sample
        gate_parts.append(lax.ppermute(of_units(w_gate, other, 1), "sample", route))
        up_parts.append(lax.ppermute(of_units(w_up, other, 1), "sample", route))
        v_unit = v_unit + lax.ppermute(of_units(own_v, other, 0), "sample", route)
    gate_parts[0] = of_units(w_gate, group, 1)
    up_parts[0] = of_units(w_up, group, 1)

    slot_is = dest_slot[None, :] == jnp.arange(all_clips, dtype=jnp.int32)[:, None]
    len_slot = jnp.sum(jnp.where(slot_is, lengths[None, :], 0), axis=1)
    my_slots = lax.dynamic_slice_in_dim(len_slot, group * clips, clips)
    edges = jnp.stack(
        [
            (band == 0).astype(jnp.int32),
            (band == n_band - 1).astype(jnp.int32),
            (stretch == 0).astype(jnp.int32),
            frame0.astype(jnp.int32),
        ]
    )
    lens = jnp.broadcast_to(my_slots[:, None], (clips, 128))
    decoded, band_sum = decode(
        edges, lens, blocks, w_in, b_in, gain_mid, w_mid, b_mid, frames, rows, widths
    )
    decoded_out = decoded.transpose(2, 0, 1, 3)

    band_sum = band_sum.reshape(n_band, frames * clips // n_band, chans)
    parts = lax.all_to_all(band_sum, "band", 0, 0, tiled=True)
    pooled = jnp.sum(parts, axis=0) / (rows * n_band * widths)
    pooled = spread(pooled.astype(jnp.bfloat16), ALL).reshape(-1, chans)
    tokens = jnp.dot(pooled, w_proj, preferred_element_type=jnp.float32).astype(jnp.bfloat16)
    token_f = tokens.astype(jnp.float32)
    normed = (
        token_f * lax.rsqrt(jnp.mean(token_f * token_f, axis=-1, keepdims=True) + 1e-06) * gain_tok
    ).astype(jnp.bfloat16)

    def product(parts):
        total = None
        for d in range(n_sample):
            source = (group - d) % n_sample
            rows_here = lax.dynamic_slice_in_dim(normed, source * depth, depth, axis=1)
            term = jnp.dot(rows_here, parts[d], preferred_element_type=jnp.float32)
            total = term if total is None else total + term
        return total

    hidden = (jax.nn.silu(product(gate_parts)) * product(up_parts)).astype(jnp.bfloat16)
    branch = jnp.sum(hidden.astype(jnp.float32) * v_unit[None, :], axis=-1)
    at_home = jnp.sum(token_f * w_score, axis=-1)
    first_device = (group == 0) & (stretch == 0) & (band == 0)
    partial = branch + jnp.where(first_device, at_home, 0.0)
    partial = partial.reshape(n_sample, n_stretch * frames, clips)
    lens_all = len_slot.reshape(n_sample, 1, clips)
    counted = jnp.arange(n_stretch * frames, dtype=jnp.int32)[None, :, None] < lens_all
    slot_part = jnp.sum(jnp.where(counted, partial, 0.0), axis=1).reshape(-1)
    slot_part = slot_part / len_slot.astype(jnp.float32)
    clip_part = jnp.sum(jnp.where(slot_is, slot_part[:, None], 0.0), axis=0)
    scores = jnp.sum(spread(clip_part, ALL), axis=0)
    return (decoded_out, scores)


def solution(mesh):
    in_specs = (
        P("sample", "stretch", "band", None),
        P(),
        P(),
        P(),
        P(),
        P(),
        P(),
        P(),
        P(),
        P(),
        P("sample", ("stretch", "band")),
        P("sample", ("stretch", "band")),
        P(("stretch", "band"), "sample"),
        P(),
    )
    out_specs = (P("sample", "stretch", "band", None), P())
    return jax.shard_map(body, mesh=mesh, in_specs=in_specs, out_specs=out_specs, check_vma=False)
```

```python
import functools

import jax
import jax.numpy as jnp
from jax import lax
from jax.experimental import pallas as pl
from jax.experimental.pallas import tpu as pltpu
from jax.sharding import PartitionSpec as P

ALL = ("sample", "stretch", "band")
TAPS = 3
BEHIND = 2 * (TAPS - 1)


def first_kernel(
    edge_ref,
    len_ref,
    *refs,
    blocks,
    frames,
    rows,
    widths,
    clips,
    chans,
):
    lat_refs = refs[:blocks]
    (w_in_ref, b_in_ref, gain_ref, w_mid_hbm, b_mid_ref) = refs[blocks : blocks + 5]
    act_hbm, first_hbm, pool_ref = refs[blocks + 5 : blocks + 8]
    x1_ref, wt_ref, sums_ref, act_ref, first_ref, wm_ref, sem = refs[blocks + 8 :]
    chans_lat = w_in_ref.shape[0] // 27
    lanes = widths * chans_lat
    frames_act = frames + TAPS - 1
    rows_act = rows + TAPS - 1
    per_frame = rows_act * clips
    weights_copy = pltpu.make_async_copy(w_mid_hbm, wm_ref, sem.at[0])
    weights_copy.start()

    skip = blocks * frames - (frames_act + TAPS - 1)

    def frame(index):
        return lat_refs[(index + skip) // frames], (index + skip) % frames

    for j in range(9):
        dt, dr = divmod(j, 3)
        for f in range(frames_act):
            ref, at = frame(f + dt)
            x1_ref[f * per_frame : (f + 1) * per_frame, j * lanes : (j + 1) * lanes] = ref[
                at, dr : dr + rows_act
            ].reshape(per_frame, lanes)
    wt_ref[...] = jnp.zeros_like(wt_ref)
    act_ref[:, :, 0] = jnp.zeros((frames_act, rows_act, clips, chans), jnp.bfloat16)
    act_ref[:, :, widths + 1] = jnp.zeros((frames_act, rows_act, clips, chans), jnp.bfloat16)

    def column(q, total_first):
        here = pl.multiple_of(q * chans_lat, chans_lat)
        before = pl.multiple_of(jnp.maximum(q - 1, 0) * chans_lat, chans_lat)
        for j in range(9):
            wt_ref[j, pl.ds(before, chans_lat), :] = jnp.zeros((chans_lat, chans), jnp.bfloat16)
            wt_ref[j, pl.ds(here, 3 * chans_lat), :] = w_in_ref[
                j * 3 * chans_lat : (j + 1) * 3 * chans_lat, :
            ]
        weight = wt_ref[:, chans_lat : chans_lat + lanes, :].reshape(9 * lanes, chans)
        total = jnp.dot(x1_ref[...], weight, preferred_element_type=jnp.float32)
        first = (total + b_in_ref[...]).astype(jnp.bfloat16)
        values = first.astype(jnp.float32)
        square = jnp.sum(values * values, axis=-1, keepdims=True) * (1.0 / chans)
        scaled = values * lax.rsqrt(square + 1e-06) * gain_ref[...]
        half = 0.5 * scaled
        act = (half + half * jnp.tanh(half)).astype(jnp.bfloat16)
        act_ref[:, :, q + 1] = act.reshape(frames_act, rows_act, clips, chans)
        inner = first.reshape(frames_act, rows_act, clips, chans)[TAPS - 1 :, 1 : 1 + rows]
        first_ref[:, :, q] = inner
        return total_first + jnp.sum(inner.astype(jnp.float32), axis=1)

    total_first = lax.fori_loop(
        0, widths, column, jnp.zeros((frames, clips, chans), jnp.float32)
    )

    @pl.when(edge_ref[0] == 1)
    def _():
        act_ref[:, 0] = jnp.zeros((frames_act, widths + 2, clips, chans), jnp.bfloat16)

    @pl.when(edge_ref[1] == 1)
    def _():
        act_ref[:, rows_act - 1] = jnp.zeros((frames_act, widths + 2, clips, chans), jnp.bfloat16)

    @pl.when(edge_ref[2] == 1)
    def _():
        act_ref[0 : TAPS - 1] = jnp.zeros(
            (TAPS - 1, rows_act, widths + 2, clips, chans), jnp.bfloat16
        )

    act_copy = pltpu.make_async_copy(act_ref, act_hbm, sem.at[1])
    first_copy = pltpu.make_async_copy(first_ref, first_hbm, sem.at[2])
    act_copy.start()
    first_copy.start()

    half_rows = frames * clips
    for f in range(frames_act):
        per_row = []
        for r in range(rows_act):
            left = act_ref[f, r, 1].astype(jnp.float32)
            right = act_ref[f, r, widths].astype(jnp.float32)
            line = left + right
            for q in range(2, widths):
                line = line + act_ref[f, r, q].astype(jnp.float32)
            per_row.append((line - right, line, line - left))
        for dr in range(TAPS):
            for dq in range(TAPS):
                box = per_row[dr][dq]
                for r in range(1, rows):
                    box = box + per_row[dr + r][dq]
                high = box.astype(jnp.bfloat16)
                low = (box - high.astype(jnp.float32)).astype(jnp.bfloat16)
                for t in range(frames):
                    dt = f - t
                    if 0 <= dt < TAPS:
                        at = ((dt * TAPS + dr) * TAPS + dq) * chans
                        sums_ref[t * clips : (t + 1) * clips, at : at + chans] = high
                        sums_ref[
                            half_rows + t * clips : half_rows + (t + 1) * clips, at : at + chans
                        ] = low

    weights_copy.wait()
    both = jnp.dot(sums_ref[...], wm_ref[...], preferred_element_type=jnp.float32)
    for t in range(frames):
        total = both[t * clips : (t + 1) * clips]
        total = total + both[half_rows + t * clips : half_rows + (t + 1) * clips]
        total = total + total_first[t] + b_mid_ref[...] * float(rows * widths)
        live = (edge_ref[3] + t) < len_ref[:, 0:1]
        pool_ref[t * clips : (t + 1) * clips, :] = jnp.where(live, total, 0.0)
    act_copy.wait()
    first_copy.wait()


def second_kernel(
    edge_ref,
    len_ref,
    act_hbm,
    first_hbm,
    wm_hbm,
    b_mid_ref,
    out_ref,
    act_ref,
    first_ref,
    wm_ref,
    act_sem,
    first_sem,
    wm_sem,
    *,
    t,
):
    rows, widths, clips, chans = first_ref.shape
    cells = rows * widths * clips
    starts = list(range(0, 27, CHUNK))
    act_copies = [
        pltpu.make_async_copy(act_hbm.at[t + dt], act_ref.at[dt], act_sem.at[dt])
        for dt in range(TAPS)
    ]
    wm_copies = []
    for i, tap in enumerate(starts):
        at = pl.ds(tap * chans, (min(tap + CHUNK, 27) - tap) * chans)
        wm_copies.append(pltpu.make_async_copy(wm_hbm.at[at], wm_ref.at[at], wm_sem.at[i]))
    first_copy = pltpu.make_async_copy(first_hbm.at[t], first_ref, first_sem)
    act_copies[0].start()
    for i, copy in enumerate(wm_copies):
        copy.start()
        if i + 1 < TAPS:
            act_copies[i + 1].start()
    first_copy.start()
    total = None
    for tap in range(0, 27, 2):
        taps = range(tap, min(tap + 2, 27))
        for k in taps:
            if k % 9 == 0:
                act_copies[k // 9].wait()
        if tap in starts:
            wm_copies[starts.index(tap)].wait()
        parts = [
            act_ref[k // 9, pl.ds((k % 9) // 3, rows), k % 3 : k % 3 + widths].reshape(cells, chans)
            for k in taps
        ]
        lhs = parts[0] if len(parts) == 1 else jnp.concatenate(parts, axis=-1)
        weight = wm_ref[tap * chans : (tap + len(parts)) * chans, :]
        term = jnp.dot(lhs, weight, preferred_element_type=jnp.float32)
        total = term if total is None else total + term
    first_copy.wait()
    live = (edge_ref[3] + t) < len_ref[:, 0:1]
    for r in range(rows):
        for q in range(widths):
            at = (r * widths + q) * clips
            mixed = (
                first_ref[r, q].astype(jnp.float32) + total[at : at + clips, :] + b_mid_ref[...]
            )
            done = jnp.where(live, mixed, 0.0).astype(jnp.bfloat16)
            out_ref[r, :, q * chans : (q + 1) * chans] = done


VMEM = pl.BlockSpec(memory_space=pltpu.VMEM)
SMEM = pl.BlockSpec(memory_space=pltpu.SMEM)
HBM = pl.BlockSpec(memory_space=pltpu.HBM)
KERNEL_VMEM = 57 * 1024 * 1024
CHUNK = 4


def first_stage(edges, lens, blocks, w_in, b_in, gain_mid, w_mid, b_mid, frames, rows, widths):
    chans = w_in.shape[1]
    clips = blocks[0].shape[2]
    lanes = blocks[0].shape[3]
    chans_lat = lanes // widths
    frames_act = frames + TAPS - 1
    rows_act = rows + TAPS - 1
    kernel = functools.partial(
        first_kernel,
        blocks=len(blocks),
        frames=frames,
        rows=rows,
        widths=widths,
        clips=clips,
        chans=chans,
    )
    return pl.pallas_call(
        kernel,
        out_shape=(
            jax.ShapeDtypeStruct((frames_act, rows_act, widths + 2, clips, chans), jnp.bfloat16),
            jax.ShapeDtypeStruct((frames, rows, widths, clips, chans), jnp.bfloat16),
            jax.ShapeDtypeStruct((frames * clips, chans), jnp.float32),
        ),
        in_specs=[SMEM, VMEM]
        + [VMEM] * len(blocks)
        + [VMEM, VMEM, VMEM, HBM, VMEM],
        out_specs=(HBM, HBM, VMEM),
        scratch_shapes=[
            pltpu.VMEM((frames_act * rows_act * clips, 9 * lanes), jnp.bfloat16),
            pltpu.VMEM((9, lanes + 2 * chans_lat, chans), jnp.bfloat16),
            pltpu.VMEM((2 * frames * clips, 27 * chans), jnp.bfloat16),
            pltpu.VMEM((frames_act, rows_act, widths + 2, clips, chans), jnp.bfloat16),
            pltpu.VMEM((frames, rows, widths, clips, chans), jnp.bfloat16),
            pltpu.VMEM(w_mid.shape, jnp.bfloat16),
            pltpu.SemaphoreType.DMA((3,)),
        ],
        compiler_params=pltpu.CompilerParams(vmem_limit_bytes=KERNEL_VMEM),
        cost_estimate=pl.CostEstimate(flops=1 << 32, bytes_accessed=1 << 16, transcendentals=0),
        name="first_stage",
    )(
        edges,
        lens,
        *blocks,
        w_in,
        b_in.reshape(1, -1),
        gain_mid.reshape(1, -1),
        w_mid,
        b_mid.reshape(1, -1),
    )


def second_stage(edges, lens, act, first, w_mid, b_mid, t):
    frames, rows, widths, clips, chans = first.shape
    flops = 2 * rows * widths * clips * chans * 27 * chans
    return pl.pallas_call(
        functools.partial(second_kernel, t=t),
        out_shape=jax.ShapeDtypeStruct((rows, clips, widths * chans), jnp.bfloat16),
        in_specs=[SMEM, VMEM, HBM, HBM, HBM, VMEM],
        out_specs=VMEM,
        scratch_shapes=[
            pltpu.VMEM((TAPS,) + act.shape[1:], jnp.bfloat16),
            pltpu.VMEM(first.shape[1:], jnp.bfloat16),
            pltpu.VMEM(w_mid.shape, jnp.bfloat16),
            pltpu.SemaphoreType.DMA((TAPS,)),
            pltpu.SemaphoreType.DMA,
            pltpu.SemaphoreType.DMA((-(-27 // CHUNK),)),
        ],
        compiler_params=pltpu.CompilerParams(vmem_limit_bytes=KERNEL_VMEM),
        cost_estimate=pl.CostEstimate(flops=flops, bytes_accessed=1 << 20, transcendentals=0),
        name="second_stage",
    )(edges, lens, act, first, w_mid, b_mid.reshape(1, -1))


def spread(value, axes):
    count = 1
    for axis in axes:
        count *= lax.axis_size(axis)
    return lax.all_to_all(
        jnp.broadcast_to(value[None], (count,) + value.shape), axes, 0, 0, tiled=True
    )


def body(
    latents,
    lengths,
    dest_slot,
    w_in,
    b_in,
    gain_mid,
    w_mid,
    b_mid,
    w_proj,
    gain_tok,
    w_gate,
    w_up,
    w_down,
    w_score,
):
    clips, frames, rows, lanes = latents.shape
    n_sample, n_stretch, n_band = (lax.axis_size(axis) for axis in ALL)
    chans_lat = w_in.shape[0] // 27
    chans = w_in.shape[1]
    widths = lanes // chans_lat
    sends = clips // n_sample
    group = lax.axis_index("sample")
    stretch = lax.axis_index("stretch")
    band = lax.axis_index("band")
    all_clips = dest_slot.shape[0]
    frame0 = stretch * frames

    my_dest = lax.dynamic_slice_in_dim(dest_slot, group * clips, clips)
    my_len = lax.dynamic_slice_in_dim(lengths, group * clips, clips)
    target = jnp.arange(n_sample, dtype=jnp.int32)[:, None] * clips + group * sends
    target = (target + jnp.arange(sends, dtype=jnp.int32)[None, :]).reshape(-1)
    select = (target[:, None] == my_dest[None, :]).astype(jnp.bfloat16)
    frame_ids = frame0 + jnp.arange(frames, dtype=jnp.int32)
    live = frame_ids[None, :] < my_len[:, None]
    masked = jnp.where(live[:, :, None, None], latents, jnp.zeros((), jnp.bfloat16))
    routed = jnp.einsum(
        "kc,ctrl->trkl", select, masked, preferred_element_type=jnp.float32
    ).astype(jnp.bfloat16)
    routed = routed.reshape(frames, rows, n_sample, sends, lanes).transpose(2, 0, 1, 3, 4)
    outgoing = jnp.broadcast_to(
        routed[:, None], (n_sample, n_band, frames, rows, sends, lanes)
    ).reshape(n_sample * n_band, frames, rows, sends, lanes)
    got = lax.all_to_all(outgoing, ("sample", "band"), 0, 0, tiled=True)
    got = got.reshape(n_sample, n_band, frames, rows, sends, lanes)
    got = got.transpose(2, 1, 3, 0, 4, 5).reshape(frames, n_band * rows, clips, lanes)
    got = jnp.pad(got, ((0, 0), (2, 2), (0, 0), (0, 0)))
    own = lax.dynamic_slice_in_dim(got, band * rows, rows + 4, axis=1)
    own, late_down = lax.optimization_barrier((own, w_down))
    hops = -(-BEHIND // frames)
    blocks = [
        lax.ppermute(own, "stretch", [(i, i + d) for i in range(n_stretch - d)])
        for d in range(hops, 0, -1)
    ] + [own]

    units = w_gate.shape[1] // n_sample

    def of_units(weight, index, axis):
        return lax.dynamic_slice_in_dim(weight, index * units, units, axis=axis)

    own_v = jnp.sum(
        late_down.astype(jnp.float32)
        * lax.dynamic_slice_in_dim(w_score, group * w_down.shape[1], w_down.shape[1])[None, :],
        axis=-1,
    )
    depth = w_gate.shape[0]
    gate_parts, up_parts, v_parts = [], [], []
    for d in range(1, n_sample):
        route = [(i, (i + d) % n_sample) for i in range(n_sample)]
        other = (group + d) % n_sample
        gate_parts.append(lax.ppermute(of_units(w_gate, other, 1), "sample", route))
        up_parts.append(lax.ppermute(of_units(w_up, other, 1), "sample", route))
        v_parts.append(lax.ppermute(of_units(own_v, other, 0), "sample", route))

    slot_is = dest_slot[None, :] == jnp.arange(all_clips, dtype=jnp.int32)[:, None]
    len_slot = jnp.sum(jnp.where(slot_is, lengths[None, :], 0), axis=1)
    my_slots = lax.dynamic_slice_in_dim(len_slot, group * clips, clips)
    edges = jnp.stack(
        [
            (band == 0).astype(jnp.int32),
            (band == n_band - 1).astype(jnp.int32),
            (stretch == 0).astype(jnp.int32),
            frame0.astype(jnp.int32),
        ]
    )
    lens = jnp.broadcast_to(my_slots[:, None], (clips, 128))
    act, first, band_sum = first_stage(
        edges, lens, blocks, w_in, b_in, gain_mid, w_mid, b_mid, frames, rows, widths
    )
    band_sum, gate_parts, up_parts, v_parts = lax.optimization_barrier(
        (band_sum, gate_parts, up_parts, v_parts)
    )
    gate_parts = [of_units(w_gate, group, 1)] + gate_parts
    up_parts = [of_units(w_up, group, 1)] + up_parts
    v_unit = of_units(own_v, group, 0) + sum(v_parts)
    decoded = [second_stage(edges, lens, act, first, w_mid, b_mid, t) for t in range(frames)]

    band_sum = band_sum.reshape(n_band, frames * clips // n_band, chans)
    parts = lax.all_to_all(band_sum, "band", 0, 0, tiled=True)
    pooled = jnp.sum(parts, axis=0) / (rows * n_band * widths)
    pooled, decoded[0] = lax.optimization_barrier((pooled, decoded[0]))
    pooled = spread(pooled.astype(jnp.bfloat16), ALL).reshape(-1, chans)
    decoded_out = jnp.stack(decoded, axis=0).transpose(2, 0, 1, 3)
    tokens = jnp.dot(pooled, w_proj, preferred_element_type=jnp.float32).astype(jnp.bfloat16)
    token_f = tokens.astype(jnp.float32)
    normed = (
        token_f * lax.rsqrt(jnp.mean(token_f * token_f, axis=-1, keepdims=True) + 1e-06) * gain_tok
    ).astype(jnp.bfloat16)

    def product(parts):
        total = None
        for d in range(n_sample):
            source = (group - d) % n_sample
            rows_here = lax.dynamic_slice_in_dim(normed, source * depth, depth, axis=1)
            term = jnp.dot(rows_here, parts[d], preferred_element_type=jnp.float32)
            total = term if total is None else total + term
        return total

    hidden = (jax.nn.silu(product(gate_parts)) * product(up_parts)).astype(jnp.bfloat16)
    branch = jnp.sum(hidden.astype(jnp.float32) * v_unit[None, :], axis=-1)
    at_home = jnp.sum(token_f * w_score, axis=-1)
    first_device = (group == 0) & (stretch == 0) & (band == 0)
    partial = branch + jnp.where(first_device, at_home, 0.0)
    partial = partial.reshape(n_sample, n_stretch * frames, clips)
    lens_all = len_slot.reshape(n_sample, 1, clips)
    counted = jnp.arange(n_stretch * frames, dtype=jnp.int32)[None, :, None] < lens_all
    slot_part = jnp.sum(jnp.where(counted, partial, 0.0), axis=1).reshape(-1)
    slot_part = slot_part / len_slot.astype(jnp.float32)
    clip_part = jnp.sum(jnp.where(slot_is, slot_part[:, None], 0.0), axis=0)
    scores = jnp.sum(spread(clip_part, ALL), axis=0)
    return (decoded_out, scores)


def solution(mesh):
    in_specs = (
        P("sample", "stretch", "band", None),
        P(),
        P(),
        P(),
        P(),
        P(),
        P(),
        P(),
        P(),
        P(),
        P("sample", ("stretch", "band")),
        P("sample", ("stretch", "band")),
        P(("stretch", "band"), "sample"),
        P(),
    )
    out_specs = (P("sample", "stretch", "band", None), P())
    return jax.shard_map(body, mesh=mesh, in_specs=in_specs, out_specs=out_specs, check_vma=False)
```

```python
import functools

import jax
import jax.numpy as jnp
from jax import lax
from jax.experimental import pallas as pl
from jax.experimental.pallas import tpu as pltpu
from jax.sharding import PartitionSpec as P

ALL = ("sample", "stretch", "band")
TAPS = 3
BEHIND = 2 * (TAPS - 1)


def decode_kernel(
    scalar_ref,
    lat_ref,
    w_in_ref,
    b_in_ref,
    gain_ref,
    w_mid_hbm,
    b_mid_ref,
    out_ref,
    pool_ref,
    x1_ref,
    wt_ref,
    act_ref,
    first_ref,
    wm_ref,
    sem,
    *,
    frames,
    rows,
    widths,
):
    clips, lanes = lat_ref.shape[2:]
    chans = w_in_ref.shape[1]
    chans_lat = w_in_ref.shape[0] // 27
    frames_act = frames + TAPS - 1
    rows_act = rows + TAPS - 1
    per_frame = rows_act * clips
    weights_copy = pltpu.make_async_copy(w_mid_hbm, wm_ref, sem)
    weights_copy.start()
    b_in = b_in_ref[...].reshape(1, chans)
    gain = gain_ref[...].reshape(1, chans)
    b_mid = b_mid_ref[...].reshape(1, chans)

    for j in range(9):
        dt, dr = divmod(j, 3)
        for f in range(frames_act):
            x1_ref[f * per_frame : (f + 1) * per_frame, j * lanes : (j + 1) * lanes] = lat_ref[
                f + dt, dr : dr + rows_act
            ].reshape(per_frame, lanes)
    wt_ref[...] = jnp.zeros_like(wt_ref)
    act_ref[:, :, 0] = jnp.zeros((frames_act, rows_act, clips, chans), jnp.bfloat16)
    act_ref[:, :, widths + 1] = jnp.zeros((frames_act, rows_act, clips, chans), jnp.bfloat16)

    def column(q, carry):
        here = pl.multiple_of(q * chans_lat, chans_lat)
        before = pl.multiple_of(jnp.maximum(q - 1, 0) * chans_lat, chans_lat)
        for j in range(9):
            wt_ref[j, pl.ds(before, chans_lat), :] = jnp.zeros((chans_lat, chans), jnp.bfloat16)
            wt_ref[j, pl.ds(here, 3 * chans_lat), :] = w_in_ref[
                j * 3 * chans_lat : (j + 1) * 3 * chans_lat, :
            ]
        weight = wt_ref[:, chans_lat : chans_lat + lanes, :].reshape(9 * lanes, chans)
        total = jnp.dot(x1_ref[...], weight, preferred_element_type=jnp.float32)
        first = (total + b_in).astype(jnp.bfloat16)
        values = first.astype(jnp.float32)
        square = jnp.sum(values * values, axis=-1, keepdims=True) * (1.0 / chans)
        half = values * lax.rsqrt(square + 1e-06) * (gain * 0.5)
        act = (half + half * jnp.tanh(half)).astype(jnp.bfloat16)
        act_ref[:, :, q + 1] = act.reshape(frames_act, rows_act, clips, chans)
        first_ref[:, :, q] = first.reshape(frames_act, rows_act, clips, chans)[
            TAPS - 1 :, 1 : 1 + rows
        ]
        return carry

    lax.fori_loop(0, widths, column, 0)

    @pl.when(scalar_ref[0] == 1)
    def _():
        act_ref[:, 0] = jnp.zeros((frames_act, widths + 2, clips, chans), jnp.bfloat16)

    @pl.when(scalar_ref[1] == 1)
    def _():
        act_ref[:, rows_act - 1] = jnp.zeros((frames_act, widths + 2, clips, chans), jnp.bfloat16)

    @pl.when(scalar_ref[2] == 1)
    def _():
        act_ref[0 : TAPS - 1] = jnp.zeros(
            (TAPS - 1, rows_act, widths + 2, clips, chans), jnp.bfloat16
        )

    weights_copy.wait()
    cells = widths * clips
    clip_ids = lax.broadcasted_iota(jnp.int32, (clips, chans), 0)
    lens = jnp.zeros((clips, chans), jnp.int32)
    for c in range(clips):
        lens = jnp.where(clip_ids == c, scalar_ref[4 + c], lens)
    pool_ref[...] = jnp.zeros_like(pool_ref)

    def line(r, carry):
        totals = [None] * frames
        for f in range(frames_act):
            outs = [t for t in range(frames) if 0 <= f - t < TAPS]
            for j in range(0, 9, 2):
                taps = range(j, min(j + 2, 9))
                lhs = [
                    act_ref[f, r + k // 3, k % 3 : k % 3 + widths].reshape(cells, chans)
                    for k in taps
                ]
                lhs = lhs[0] if len(lhs) == 1 else jnp.concatenate(lhs, axis=-1)
                weights = []
                for t in outs:
                    at = (f - t) * 9 + j
                    weights.append(wm_ref[at * chans : (at + len(taps)) * chans, :])
                weight = weights[0] if len(outs) == 1 else jnp.concatenate(weights, axis=-1)
                term = jnp.dot(lhs, weight, preferred_element_type=jnp.float32)
                for i, t in enumerate(outs):
                    part = term[:, i * chans : (i + 1) * chans]
                    totals[t] = part if totals[t] is None else totals[t] + part
        for t in range(frames):
            live = (scalar_ref[3] + t) < lens
            pooled = pool_ref[t]
            for q in range(widths):
                mixed = (
                    first_ref[t, r, q].astype(jnp.float32)
                    + totals[t][q * clips : (q + 1) * clips, :]
                    + b_mid
                )
                done = jnp.where(live, mixed, 0.0).astype(jnp.bfloat16)
                out_ref[t, r, :, q * chans : (q + 1) * chans] = done
                pooled = pooled + done.astype(jnp.float32)
            pool_ref[t] = pooled
        return carry

    lax.fori_loop(0, rows, line, 0)


VMEM = pl.BlockSpec(memory_space=pltpu.VMEM)
SMEM = pl.BlockSpec(memory_space=pltpu.SMEM)
HBM = pl.BlockSpec(memory_space=pltpu.HBM)
KERNEL_VMEM = 57 * 1024 * 1024


def decode(scalars, cells, w_in, b_in, gain_mid, w_mid, b_mid, frames, rows, widths):
    chans = w_in.shape[1]
    clips, lanes = cells.shape[2:]
    chans_lat = lanes // widths
    frames_act = frames + TAPS - 1
    rows_act = rows + TAPS - 1
    flops = 2 * frames * rows * widths * clips * chans * 27 * chans
    return pl.pallas_call(
        functools.partial(decode_kernel, frames=frames, rows=rows, widths=widths),
        out_shape=(
            jax.ShapeDtypeStruct((frames, rows, clips, widths * chans), jnp.bfloat16),
            jax.ShapeDtypeStruct((frames, clips, chans), jnp.float32),
        ),
        in_specs=[SMEM, VMEM, VMEM, VMEM, VMEM, HBM, VMEM],
        out_specs=(VMEM, VMEM),
        scratch_shapes=[
            pltpu.VMEM((frames_act * rows_act * clips, 9 * lanes), jnp.bfloat16),
            pltpu.VMEM((9, lanes + 2 * chans_lat, chans), jnp.bfloat16),
            pltpu.VMEM((frames_act, rows_act, widths + 2, clips, chans), jnp.bfloat16),
            pltpu.VMEM((frames, rows, widths, clips, chans), jnp.bfloat16),
            pltpu.VMEM(w_mid.shape, jnp.bfloat16),
            pltpu.SemaphoreType.DMA,
        ],
        compiler_params=pltpu.CompilerParams(vmem_limit_bytes=KERNEL_VMEM),
        cost_estimate=pl.CostEstimate(flops=flops, bytes_accessed=1 << 16, transcendentals=0),
        name="decode",
    )(scalars, cells, w_in, b_in, gain_mid, w_mid, b_mid)


def spread(value, axes):
    count = 1
    for axis in axes:
        count *= lax.axis_size(axis)
    return lax.all_to_all(
        jnp.broadcast_to(value[None], (count,) + value.shape), axes, 0, 0, tiled=True
    )


def body(
    latents,
    lengths,
    dest_slot,
    w_in,
    b_in,
    gain_mid,
    w_mid,
    b_mid,
    w_proj,
    gain_tok,
    w_gate,
    w_up,
    w_down,
    w_score,
):
    clips, frames, rows, lanes = latents.shape
    n_sample, n_stretch, n_band = (lax.axis_size(axis) for axis in ALL)
    chans_lat = w_in.shape[0] // 27
    chans = w_in.shape[1]
    widths = lanes // chans_lat
    sends = clips // n_sample
    group = lax.axis_index("sample")
    stretch = lax.axis_index("stretch")
    band = lax.axis_index("band")
    all_clips = dest_slot.shape[0]
    frame0 = stretch * frames

    hops = -(-BEHIND // frames)
    series = [
        lax.ppermute(latents, "stretch", [(i, i + d) for i in range(n_stretch - d)])
        for d in range(hops, 0, -1)
    ] + [latents]
    series = jnp.concatenate(series, axis=1)[:, hops * frames - BEHIND :]
    all_frames = frames + BEHIND
    is_group = jnp.arange(n_sample, dtype=jnp.int32)[:, None] == group
    my_dest = jnp.sum(jnp.where(is_group, dest_slot.reshape(n_sample, clips), 0), axis=0)
    my_len = jnp.sum(jnp.where(is_group, lengths.reshape(n_sample, clips), 0), axis=0)
    target = jnp.arange(n_sample, dtype=jnp.int32)[:, None] * clips + group * sends
    target = (target + jnp.arange(sends, dtype=jnp.int32)[None, :]).reshape(-1)
    select = (target[:, None] == my_dest[None, :]).astype(jnp.bfloat16)
    frame_ids = frame0 - BEHIND + jnp.arange(all_frames, dtype=jnp.int32)
    live = frame_ids[None, :] < my_len[:, None]
    masked = jnp.where(live[:, :, None, None], series, jnp.zeros((), jnp.bfloat16))
    routed = jnp.einsum(
        "kc,ctrl->trkl", select, masked, preferred_element_type=jnp.float32
    ).astype(jnp.bfloat16)
    routed = routed.reshape(all_frames, rows, n_sample, sends, lanes).transpose(2, 0, 1, 3, 4)
    outgoing = jnp.broadcast_to(
        routed[:, None], (n_sample, n_band, all_frames, rows, sends, lanes)
    ).reshape(n_sample * n_band, all_frames, rows, sends, lanes)
    got = lax.all_to_all(outgoing, ("sample", "band"), 0, 0, tiled=True)
    got = got.reshape(n_sample, n_band, all_frames, rows, sends, lanes)
    got = got.transpose(2, 1, 3, 0, 4, 5).reshape(all_frames, n_band * rows, clips, lanes)
    got = jnp.pad(got, ((0, 0), (2, 2), (0, 0), (0, 0)))
    cells = lax.dynamic_slice_in_dim(got, band * rows, rows + 4, axis=1)

    units = w_gate.shape[1] // n_sample

    def of_units(weight, index, axis):
        return lax.dynamic_slice_in_dim(weight, index * units, units, axis=axis)

    own_v = jnp.sum(
        w_down.astype(jnp.float32)
        * lax.dynamic_slice_in_dim(w_score, group * w_down.shape[1], w_down.shape[1])[None, :],
        axis=-1,
    )
    depth = w_gate.shape[0]
    gate_parts, up_parts, v_parts = [], [], []
    for d in range(1, n_sample):
        route = [(i, (i + d) % n_sample) for i in range(n_sample)]
        other = (group + d) % n_sample
        gate_parts.append(lax.ppermute(of_units(w_gate, other, 1), "sample", route))
        up_parts.append(lax.ppermute(of_units(w_up, other, 1), "sample", route))
        v_parts.append(lax.ppermute(of_units(own_v, other, 0), "sample", route))

    slot_is = dest_slot[None, :] == jnp.arange(all_clips, dtype=jnp.int32)[:, None]
    len_slot = jnp.sum(jnp.where(slot_is, lengths[None, :], 0), axis=1)
    my_slots = lax.dynamic_slice_in_dim(len_slot, group * clips, clips)
    scalars = jnp.concatenate(
        [
            jnp.stack([band == 0, band == n_band - 1, stretch == 0]).astype(jnp.int32),
            frame0[None].astype(jnp.int32),
            my_slots,
        ]
    )
    decoded, band_sum = decode(
        scalars, cells, w_in, b_in, gain_mid, w_mid, b_mid, frames, rows, widths
    )
    band_sum, gate_parts, up_parts, v_parts = lax.optimization_barrier(
        (band_sum, gate_parts, up_parts, v_parts)
    )
    gate_parts = [of_units(w_gate, group, 1)] + gate_parts
    up_parts = [of_units(w_up, group, 1)] + up_parts
    v_unit = of_units(own_v, group, 0) + sum(v_parts)
    decoded_out = decoded.transpose(2, 0, 1, 3)

    band_sum = band_sum.reshape(n_band, frames * clips // n_band, chans)
    parts = lax.all_to_all(band_sum, "band", 0, 0, tiled=True)
    pooled = jnp.sum(parts, axis=0) / (rows * n_band * widths)
    pooled = spread(pooled.astype(jnp.bfloat16), ALL).reshape(-1, chans)
    tokens = jnp.dot(pooled, w_proj, preferred_element_type=jnp.float32).astype(jnp.bfloat16)
    token_f = tokens.astype(jnp.float32)
    normed = (
        token_f * lax.rsqrt(jnp.mean(token_f * token_f, axis=-1, keepdims=True) + 1e-06) * gain_tok
    ).astype(jnp.bfloat16)

    def product(parts):
        total = None
        for d in range(n_sample):
            source = (group - d) % n_sample
            rows_here = lax.dynamic_slice_in_dim(normed, source * depth, depth, axis=1)
            term = jnp.dot(rows_here, parts[d], preferred_element_type=jnp.float32)
            total = term if total is None else total + term
        return total

    hidden = (jax.nn.silu(product(gate_parts)) * product(up_parts)).astype(jnp.bfloat16)
    branch = jnp.sum(hidden.astype(jnp.float32) * v_unit[None, :], axis=-1)
    at_home = jnp.sum(token_f * w_score, axis=-1)
    first_device = (group == 0) & (stretch == 0) & (band == 0)
    partial = branch + jnp.where(first_device, at_home, 0.0)
    partial = partial.reshape(n_sample, n_stretch * frames, clips)
    lens_all = len_slot.reshape(n_sample, 1, clips)
    counted = jnp.arange(n_stretch * frames, dtype=jnp.int32)[None, :, None] < lens_all
    slot_part = jnp.sum(jnp.where(counted, partial, 0.0), axis=1).reshape(-1)
    slot_part = slot_part / len_slot.astype(jnp.float32)
    clip_part = jnp.sum(jnp.where(slot_is, slot_part[:, None], 0.0), axis=0)
    scores = jnp.sum(spread(clip_part, ALL), axis=0)
    return (decoded_out, scores)


def solution(mesh):
    in_specs = (
        P("sample", "stretch", "band", None),
        P(),
        P(),
        P(),
        P(),
        P(),
        P(),
        P(),
        P(),
        P(),
        P("sample", ("stretch", "band")),
        P("sample", ("stretch", "band")),
        P(("stretch", "band"), "sample"),
        P(),
    )
    out_specs = (P("sample", "stretch", "band", None), P())
    return jax.shard_map(body, mesh=mesh, in_specs=in_specs, out_specs=out_specs, check_vma=False)
```

```python
import functools

import jax
import jax.numpy as jnp
from jax import lax
from jax.experimental import pallas as pl
from jax.experimental.pallas import tpu as pltpu
from jax.sharding import PartitionSpec as P

ALL = ("sample", "stretch", "band")
TAPS = 3
BEHIND = 2 * (TAPS - 1)


def decode_kernel(
    scalar_ref,
    lat_ref,
    w_in_ref,
    b_in_ref,
    gain_ref,
    w_mid_hbm,
    b_mid_ref,
    out_ref,
    pool_ref,
    x1_ref,
    wt_ref,
    act_ref,
    first_ref,
    wm_ref,
    sem,
    *,
    frames,
    rows,
    widths,
):
    clips, lanes = lat_ref.shape[2:]
    chans = w_in_ref.shape[1]
    chans_lat = w_in_ref.shape[0] // 27
    frames_act = frames + TAPS - 1
    rows_act = rows + TAPS - 1
    per_frame = rows_act * clips
    weights_copy = pltpu.make_async_copy(w_mid_hbm, wm_ref, sem)
    weights_copy.start()
    b_in = b_in_ref[...].reshape(1, chans)
    gain = gain_ref[...].reshape(1, chans)
    b_mid = b_mid_ref[...].reshape(1, chans)

    for j in range(9):
        dt, dr = divmod(j, 3)
        for f in range(frames_act):
            x1_ref[f * per_frame : (f + 1) * per_frame, j * lanes : (j + 1) * lanes] = lat_ref[
                f + dt, dr : dr + rows_act
            ].reshape(per_frame, lanes)
    wt_ref[...] = jnp.zeros_like(wt_ref)
    for q in range(widths):
        for j in range(9):
            wt_ref[q, j, q * chans_lat : (q + 3) * chans_lat, :] = w_in_ref[
                j * 3 * chans_lat : (j + 1) * 3 * chans_lat, :
            ]
    act_ref[:, :, 0] = jnp.zeros((frames_act, rows_act, clips, chans), jnp.bfloat16)
    act_ref[:, :, widths + 1] = jnp.zeros((frames_act, rows_act, clips, chans), jnp.bfloat16)

    def column(q, carry):
        weight = wt_ref[q, :, chans_lat : chans_lat + lanes, :].reshape(9 * lanes, chans)
        total = jnp.dot(x1_ref[...], weight, preferred_element_type=jnp.float32)
        first = (total + b_in).astype(jnp.bfloat16)
        values = first.astype(jnp.float32)
        square = jnp.sum(values * values, axis=-1, keepdims=True) * (1.0 / chans)
        half = values * lax.rsqrt(square + 1e-06) * (gain * 0.5)
        act = (half + half * jnp.tanh(half)).astype(jnp.bfloat16)
        act_ref[:, :, q + 1] = act.reshape(frames_act, rows_act, clips, chans)
        first_ref[:, :, q] = first.reshape(frames_act, rows_act, clips, chans)[
            TAPS - 1 :, 1 : 1 + rows
        ]
        return carry

    lax.fori_loop(0, widths, column, 0, unroll=True)

    @pl.when(scalar_ref[0] == 1)
    def _():
        act_ref[:, 0] = jnp.zeros((frames_act, widths + 2, clips, chans), jnp.bfloat16)

    @pl.when(scalar_ref[1] == 1)
    def _():
        act_ref[:, rows_act - 1] = jnp.zeros((frames_act, widths + 2, clips, chans), jnp.bfloat16)

    @pl.when(scalar_ref[2] == 1)
    def _():
        act_ref[0 : TAPS - 1] = jnp.zeros(
            (TAPS - 1, rows_act, widths + 2, clips, chans), jnp.bfloat16
        )

    weights_copy.wait()
    cells = widths * clips
    clip_ids = lax.broadcasted_iota(jnp.int32, (clips, chans), 0)
    lens = jnp.zeros((clips, chans), jnp.int32)
    for c in range(clips):
        lens = jnp.where(clip_ids == c, scalar_ref[4 + c], lens)
    pool_ref[...] = jnp.zeros_like(pool_ref)

    def line(r, carry):
        totals = [None] * frames
        for f in range(frames_act):
            outs = [t for t in range(frames) if 0 <= f - t < TAPS]
            for j in range(0, 9, 2):
                taps = range(j, min(j + 2, 9))
                lhs = [
                    act_ref[f, r + k // 3, k % 3 : k % 3 + widths].reshape(cells, chans)
                    for k in taps
                ]
                lhs = lhs[0] if len(lhs) == 1 else jnp.concatenate(lhs, axis=-1)
                weights = []
                for t in outs:
                    at = (f - t) * 9 + j
                    weights.append(wm_ref[at * chans : (at + len(taps)) * chans, :])
                weight = weights[0] if len(outs) == 1 else jnp.concatenate(weights, axis=-1)
                term = jnp.dot(lhs, weight, preferred_element_type=jnp.float32)
                for i, t in enumerate(outs):
                    part = term[:, i * chans : (i + 1) * chans]
                    totals[t] = part if totals[t] is None else totals[t] + part
        for t in range(frames):
            live = (scalar_ref[3] + t) < lens
            pooled = pool_ref[t]
            for q in range(widths):
                mixed = (
                    first_ref[t, r, q].astype(jnp.float32)
                    + totals[t][q * clips : (q + 1) * clips, :]
                    + b_mid
                )
                done = jnp.where(live, mixed, 0.0).astype(jnp.bfloat16)
                out_ref[t, r, :, q * chans : (q + 1) * chans] = done
                pooled = pooled + done.astype(jnp.float32)
            pool_ref[t] = pooled
        return carry

    lax.fori_loop(0, rows, line, 0, unroll=2)


VMEM = pl.BlockSpec(memory_space=pltpu.VMEM)
SMEM = pl.BlockSpec(memory_space=pltpu.SMEM)
HBM = pl.BlockSpec(memory_space=pltpu.HBM)
KERNEL_VMEM = 57 * 1024 * 1024


def decode(scalars, cells, w_in, b_in, gain_mid, w_mid, b_mid, frames, rows, widths):
    chans = w_in.shape[1]
    clips, lanes = cells.shape[2:]
    chans_lat = lanes // widths
    frames_act = frames + TAPS - 1
    rows_act = rows + TAPS - 1
    flops = 2 * frames * rows * widths * clips * chans * 27 * chans
    return pl.pallas_call(
        functools.partial(decode_kernel, frames=frames, rows=rows, widths=widths),
        out_shape=(
            jax.ShapeDtypeStruct((frames, rows, clips, widths * chans), jnp.bfloat16),
            jax.ShapeDtypeStruct((frames, clips, chans), jnp.float32),
        ),
        in_specs=[SMEM, VMEM, VMEM, VMEM, VMEM, HBM, VMEM],
        out_specs=(VMEM, VMEM),
        scratch_shapes=[
            pltpu.VMEM((frames_act * rows_act * clips, 9 * lanes), jnp.bfloat16),
            pltpu.VMEM((widths, 9, lanes + 2 * chans_lat, chans), jnp.bfloat16),
            pltpu.VMEM((frames_act, rows_act, widths + 2, clips, chans), jnp.bfloat16),
            pltpu.VMEM((frames, rows, widths, clips, chans), jnp.bfloat16),
            pltpu.VMEM(w_mid.shape, jnp.bfloat16),
            pltpu.SemaphoreType.DMA,
        ],
        compiler_params=pltpu.CompilerParams(vmem_limit_bytes=KERNEL_VMEM),
        cost_estimate=pl.CostEstimate(flops=flops, bytes_accessed=1 << 16, transcendentals=0),
        name="decode",
    )(scalars, cells, w_in, b_in, gain_mid, w_mid, b_mid)


def spread(value, axes):
    count = 1
    for axis in axes:
        count *= lax.axis_size(axis)
    return lax.all_to_all(
        jnp.broadcast_to(value[None], (count,) + value.shape), axes, 0, 0, tiled=True
    )


def body(
    latents,
    lengths,
    dest_slot,
    w_in,
    b_in,
    gain_mid,
    w_mid,
    b_mid,
    w_proj,
    gain_tok,
    w_gate,
    w_up,
    w_down,
    w_score,
):
    clips, frames, rows, lanes = latents.shape
    n_sample, n_stretch, n_band = (lax.axis_size(axis) for axis in ALL)
    chans_lat = w_in.shape[0] // 27
    chans = w_in.shape[1]
    widths = lanes // chans_lat
    sends = clips // n_sample
    group = lax.axis_index("sample")
    stretch = lax.axis_index("stretch")
    band = lax.axis_index("band")
    all_clips = dest_slot.shape[0]
    frame0 = stretch * frames

    hops = -(-BEHIND // frames)
    series = [
        lax.ppermute(latents, "stretch", [(i, i + d) for i in range(n_stretch - d)])
        for d in range(hops, 0, -1)
    ] + [latents]
    series = jnp.concatenate(series, axis=1)[:, hops * frames - BEHIND :]
    all_frames = frames + BEHIND
    ids = jnp.arange(all_clips, dtype=jnp.int32)
    mine = ids[None, :] == (group * clips + jnp.arange(clips, dtype=jnp.int32))[:, None]
    my_dest = jnp.sum(jnp.where(mine, dest_slot[None, :], 0), axis=1)
    my_len = jnp.sum(jnp.where(mine, lengths[None, :], 0), axis=1)
    target = jnp.arange(n_sample, dtype=jnp.int32)[:, None] * clips + group * sends
    target = (target + jnp.arange(sends, dtype=jnp.int32)[None, :]).reshape(-1)
    select = (target[:, None] == my_dest[None, :]).astype(jnp.bfloat16)
    frame_ids = frame0 - BEHIND + jnp.arange(all_frames, dtype=jnp.int32)
    live = frame_ids[None, :] < my_len[:, None]
    masked = jnp.where(live[:, :, None, None], series, jnp.zeros((), jnp.bfloat16))
    routed = jnp.einsum(
        "kc,ctrl->trkl", select, masked, preferred_element_type=jnp.float32
    ).astype(jnp.bfloat16)
    routed = routed.reshape(all_frames, rows, n_sample, sends, lanes).transpose(2, 0, 1, 3, 4)
    outgoing = jnp.broadcast_to(
        routed[:, None], (n_sample, n_band, all_frames, rows, sends, lanes)
    ).reshape(n_sample * n_band, all_frames, rows, sends, lanes)
    units = w_gate.shape[1] // n_sample

    def of_units(weight, index, axis):
        return lax.dynamic_slice_in_dim(weight, index * units, units, axis=axis)

    others = [(group + d) % n_sample for d in range(1, n_sample)]
    outbound = [
        jnp.concatenate([of_units(w_gate.T, i, 0), of_units(w_up.T, i, 0)], axis=0) for i in others
    ]
    outgoing, outbound = lax.optimization_barrier((outgoing, outbound))
    got = lax.all_to_all(outgoing, ("sample", "band"), 0, 0, tiled=True)
    got = got.reshape(n_sample, n_band, all_frames, rows, sends, lanes)
    got = got.transpose(2, 1, 3, 0, 4, 5).reshape(all_frames, n_band * rows, clips, lanes)
    got = jnp.pad(got, ((0, 0), (2, 2), (0, 0), (0, 0)))
    cells = lax.dynamic_slice_in_dim(got, band * rows, rows + 4, axis=1)

    own_v = jnp.sum(
        w_down.astype(jnp.float32)
        * lax.dynamic_slice_in_dim(w_score, group * w_down.shape[1], w_down.shape[1])[None, :],
        axis=-1,
    )
    depth = w_gate.shape[0]
    arrived, v_parts = [], []
    for d in range(1, n_sample):
        route = [(i, (i + d) % n_sample) for i in range(n_sample)]
        arrived.append(lax.ppermute(outbound[d - 1], "sample", route))
        v_parts.append(lax.ppermute(of_units(own_v, others[d - 1], 0), "sample", route))

    slot_is = dest_slot[None, :] == jnp.arange(all_clips, dtype=jnp.int32)[:, None]
    len_slot = jnp.sum(jnp.where(slot_is, lengths[None, :], 0), axis=1)
    my_slots = lax.dynamic_slice_in_dim(len_slot, group * clips, clips)
    scalars = jnp.concatenate(
        [
            jnp.stack([band == 0, band == n_band - 1, stretch == 0]).astype(jnp.int32),
            frame0[None].astype(jnp.int32),
            my_slots,
        ]
    )
    decoded, band_sum = decode(
        scalars, cells, w_in, b_in, gain_mid, w_mid, b_mid, frames, rows, widths
    )
    decoded_out = decoded.transpose(2, 0, 1, 3)

    band_sum, v_parts = lax.optimization_barrier((band_sum, v_parts))
    band_sum = band_sum.reshape(n_band, frames * clips // n_band, chans)
    parts = lax.all_to_all(band_sum, "band", 0, 0, tiled=True)
    pooled = jnp.sum(parts, axis=0) / (rows * n_band * widths)
    pooled, arrived = lax.optimization_barrier((pooled, arrived))
    gate_parts = [of_units(w_gate, group, 1)] + [w[:units].T for w in arrived]
    up_parts = [of_units(w_up, group, 1)] + [w[units:].T for w in arrived]
    v_unit = of_units(own_v, group, 0) + sum(v_parts)
    pooled = spread(pooled.astype(jnp.bfloat16), ALL).reshape(-1, chans)
    tokens = jnp.dot(pooled, w_proj, preferred_element_type=jnp.float32).astype(jnp.bfloat16)
    token_f = tokens.astype(jnp.float32)
    normed = (
        token_f * lax.rsqrt(jnp.mean(token_f * token_f, axis=-1, keepdims=True) + 1e-06) * gain_tok
    ).astype(jnp.bfloat16)

    def product(parts):
        total = None
        for d in range(n_sample):
            source = (group - d) % n_sample
            rows_here = lax.dynamic_slice_in_dim(normed, source * depth, depth, axis=1)
            term = jnp.dot(rows_here, parts[d], preferred_element_type=jnp.float32)
            total = term if total is None else total + term
        return total

    hidden = (jax.nn.silu(product(gate_parts)) * product(up_parts)).astype(jnp.bfloat16)
    branch = jnp.sum(hidden.astype(jnp.float32) * v_unit[None, :], axis=-1)
    at_home = jnp.sum(token_f * w_score, axis=-1)
    first_device = (group == 0) & (stretch == 0) & (band == 0)
    partial = branch + jnp.where(first_device, at_home, 0.0)
    partial = partial.reshape(n_sample, n_stretch * frames, clips)
    lens_all = len_slot.reshape(n_sample, 1, clips)
    counted = jnp.arange(n_stretch * frames, dtype=jnp.int32)[None, :, None] < lens_all
    slot_part = jnp.sum(jnp.where(counted, partial, 0.0), axis=1).reshape(-1)
    slot_part = slot_part / len_slot.astype(jnp.float32)
    clip_part = jnp.sum(jnp.where(slot_is, slot_part[:, None], 0.0), axis=0)
    scores = jnp.sum(spread(clip_part, ALL), axis=0)
    return (decoded_out, scores)


def solution(mesh):
    in_specs = (
        P("sample", "stretch", "band", None),
        P(),
        P(),
        P(),
        P(),
        P(),
        P(),
        P(),
        P(),
        P(),
        P("sample", ("stretch", "band")),
        P("sample", ("stretch", "band")),
        P(("stretch", "band"), "sample"),
        P(),
    )
    out_specs = (P("sample", "stretch", "band", None), P())
    return jax.shard_map(body, mesh=mesh, in_specs=in_specs, out_specs=out_specs, check_vma=False)
```

```python
import functools

import jax
import jax.numpy as jnp
from jax import lax
from jax.experimental import pallas as pl
from jax.experimental.pallas import tpu as pltpu
from jax.sharding import PartitionSpec as P

ALL = ("sample", "stretch", "band")
TAPS = 3
BEHIND = 2 * (TAPS - 1)
STEP = 2


def decode_kernel(
    scalar_ref,
    lat_ref,
    w_in_ref,
    b_in_ref,
    gain_ref,
    w_mid_hbm,
    b_mid_ref,
    out_ref,
    pool_ref,
    x1_ref,
    wt_ref,
    act_ref,
    first_ref,
    wm_ref,
    sem,
    *,
    frames,
    rows,
    widths,
):
    clips, lanes = lat_ref.shape[2:]
    chans = w_in_ref.shape[1]
    chans_lat = w_in_ref.shape[0] // 27
    frames_act = frames + TAPS - 1
    rows_act = rows + TAPS - 1
    per_frame = rows_act * clips
    weights_copy = pltpu.make_async_copy(w_mid_hbm, wm_ref, sem)
    weights_copy.start()
    b_in = b_in_ref[...].reshape(1, chans)
    gain = gain_ref[...].reshape(1, chans)
    b_mid = b_mid_ref[...].reshape(1, chans)

    for j in range(9):
        dt, dr = divmod(j, 3)
        for f in range(frames_act):
            x1_ref[f * per_frame : (f + 1) * per_frame, j * lanes : (j + 1) * lanes] = lat_ref[
                f + dt, dr : dr + rows_act
            ].reshape(per_frame, lanes)
    wt_ref[...] = jnp.zeros_like(wt_ref)
    middle = lanes - chans_lat
    for j in range(9):
        wt_ref[j, middle : middle + 3 * chans_lat, :] = w_in_ref[
            j * 3 * chans_lat : (j + 1) * 3 * chans_lat, :
        ]
    act_ref[:, :, 0] = jnp.zeros((frames_act, rows_act, clips, chans), jnp.bfloat16)
    act_ref[:, :, widths + 1] = jnp.zeros((frames_act, rows_act, clips, chans), jnp.bfloat16)

    def column(q, carry):
        at = pl.multiple_of(lanes - q * chans_lat, chans_lat)
        weight = wt_ref[:, pl.ds(at, lanes), :].reshape(9 * lanes, chans)
        total = jnp.dot(x1_ref[...], weight, preferred_element_type=jnp.float32)
        first = (total + b_in).astype(jnp.bfloat16)
        values = first.astype(jnp.float32)
        square = jnp.sum(values * values, axis=-1, keepdims=True) * (1.0 / chans)
        half = values * lax.rsqrt(square + 1e-06) * (gain * 0.5)
        act = (half + half * jnp.tanh(half)).astype(jnp.bfloat16)
        act_ref[:, :, q + 1] = act.reshape(frames_act, rows_act, clips, chans)
        first_ref[:, :, q] = first.reshape(frames_act, rows_act, clips, chans)[
            TAPS - 1 :, 1 : 1 + rows
        ]
        return carry

    lax.fori_loop(0, widths, column, 0, unroll=True)

    @pl.when(scalar_ref[0] == 1)
    def _():
        act_ref[:, 0] = jnp.zeros((frames_act, widths + 2, clips, chans), jnp.bfloat16)

    @pl.when(scalar_ref[1] == 1)
    def _():
        act_ref[:, rows_act - 1] = jnp.zeros((frames_act, widths + 2, clips, chans), jnp.bfloat16)

    @pl.when(scalar_ref[2] == 1)
    def _():
        act_ref[0 : TAPS - 1] = jnp.zeros(
            (TAPS - 1, rows_act, widths + 2, clips, chans), jnp.bfloat16
        )

    weights_copy.wait()
    cells = STEP * widths * clips
    clip_ids = lax.broadcasted_iota(jnp.int32, (clips, chans), 0)
    lens = jnp.zeros((clips, chans), jnp.int32)
    for c in range(clips):
        lens = jnp.where(clip_ids == c, scalar_ref[4 + c], lens)
    pool_ref[...] = jnp.zeros_like(pool_ref)

    def line(r, carry):
        totals = [None] * frames
        for f in range(frames_act):
            outs = [t for t in range(frames) if 0 <= f - t < TAPS]
            for j in range(0, 9, 9):
                taps = range(j, min(j + 9, 9))
                lhs = [
                    act_ref[
                        f, pl.ds(r * STEP + k // 3, STEP), k % 3 : k % 3 + widths
                    ].reshape(cells, chans)
                    for k in taps
                ]
                lhs = lhs[0] if len(lhs) == 1 else jnp.concatenate(lhs, axis=-1)
                weights = []
                for t in outs:
                    at = (f - t) * 9 + j
                    weights.append(wm_ref[at * chans : (at + len(taps)) * chans, :])
                weight = weights[0] if len(outs) == 1 else jnp.concatenate(weights, axis=-1)
                term = jnp.dot(lhs, weight, preferred_element_type=jnp.float32)
                for i, t in enumerate(outs):
                    part = term[:, i * chans : (i + 1) * chans]
                    totals[t] = part if totals[t] is None else totals[t] + part
        for t in range(frames):
            live = (scalar_ref[3] + t) < lens
            pooled = pool_ref[t]
            for i in range(STEP * widths):
                line_at, q = divmod(i, widths)
                mixed = (
                    first_ref[t, r * STEP + line_at, q].astype(jnp.float32)
                    + totals[t][i * clips : (i + 1) * clips, :]
                    + b_mid
                )
                done = jnp.where(live, mixed, 0.0).astype(jnp.bfloat16)
                out_ref[t, r * STEP + line_at, :, q * chans : (q + 1) * chans] = done
                pooled = pooled + done.astype(jnp.float32)
            pool_ref[t] = pooled
        return carry

    lax.fori_loop(0, rows // STEP, line, 0)


VMEM = pl.BlockSpec(memory_space=pltpu.VMEM)
SMEM = pl.BlockSpec(memory_space=pltpu.SMEM)
HBM = pl.BlockSpec(memory_space=pltpu.HBM)
KERNEL_VMEM = 57 * 1024 * 1024


def decode(scalars, cells, w_in, b_in, gain_mid, w_mid, b_mid, frames, rows, widths):
    chans = w_in.shape[1]
    clips, lanes = cells.shape[2:]
    chans_lat = lanes // widths
    frames_act = frames + TAPS - 1
    rows_act = rows + TAPS - 1
    flops = 2 * frames * rows * widths * clips * chans * 27 * chans
    return pl.pallas_call(
        functools.partial(decode_kernel, frames=frames, rows=rows, widths=widths),
        out_shape=(
            jax.ShapeDtypeStruct((frames, rows, clips, widths * chans), jnp.bfloat16),
            jax.ShapeDtypeStruct((frames, clips, chans), jnp.float32),
        ),
        in_specs=[SMEM, VMEM, VMEM, VMEM, VMEM, HBM, VMEM],
        out_specs=(VMEM, VMEM),
        scratch_shapes=[
            pltpu.VMEM((frames_act * rows_act * clips, 9 * lanes), jnp.bfloat16),
            pltpu.VMEM((9, 2 * lanes, chans), jnp.bfloat16),
            pltpu.VMEM((frames_act, rows_act, widths + 2, clips, chans), jnp.bfloat16),
            pltpu.VMEM((frames, rows, widths, clips, chans), jnp.bfloat16),
            pltpu.VMEM(w_mid.shape, jnp.bfloat16),
            pltpu.SemaphoreType.DMA,
        ],
        compiler_params=pltpu.CompilerParams(vmem_limit_bytes=KERNEL_VMEM),
        cost_estimate=pl.CostEstimate(flops=flops, bytes_accessed=1 << 16, transcendentals=0),
        name="decode",
    )(scalars, cells, w_in, b_in, gain_mid, w_mid, b_mid)


def spread(value, axes):
    count = 1
    for axis in axes:
        count *= lax.axis_size(axis)
    return lax.all_to_all(
        jnp.broadcast_to(value[None], (count,) + value.shape), axes, 0, 0, tiled=True
    )


def body(
    latents,
    lengths,
    dest_slot,
    w_in,
    b_in,
    gain_mid,
    w_mid,
    b_mid,
    w_proj,
    gain_tok,
    w_gate,
    w_up,
    w_down,
    w_score,
):
    clips, frames, rows, lanes = latents.shape
    n_sample, n_stretch, n_band = (lax.axis_size(axis) for axis in ALL)
    chans_lat = w_in.shape[0] // 27
    chans = w_in.shape[1]
    widths = lanes // chans_lat
    sends = clips // n_sample
    group = lax.axis_index("sample")
    stretch = lax.axis_index("stretch")
    band = lax.axis_index("band")
    all_clips = dest_slot.shape[0]
    frame0 = stretch * frames

    hops = -(-BEHIND // frames)
    series = [
        lax.ppermute(latents, "stretch", [(i, i + d) for i in range(n_stretch - d)])
        for d in range(hops, 0, -1)
    ] + [latents]
    series = jnp.concatenate(series, axis=1)[:, hops * frames - BEHIND :]
    all_frames = frames + BEHIND
    ids = jnp.arange(all_clips, dtype=jnp.int32)
    mine = ids[None, :] == (group * clips + jnp.arange(clips, dtype=jnp.int32))[:, None]
    my_dest = jnp.sum(jnp.where(mine, dest_slot[None, :], 0), axis=1)
    my_len = jnp.sum(jnp.where(mine, lengths[None, :], 0), axis=1)
    target = jnp.arange(n_sample, dtype=jnp.int32)[:, None] * clips + group * sends
    target = (target + jnp.arange(sends, dtype=jnp.int32)[None, :]).reshape(-1)
    select = (target[:, None] == my_dest[None, :]).astype(jnp.bfloat16)
    frame_ids = frame0 - BEHIND + jnp.arange(all_frames, dtype=jnp.int32)
    live = frame_ids[None, :] < my_len[:, None]
    masked = jnp.where(live[:, :, None, None], series, jnp.zeros((), jnp.bfloat16))
    routed = jnp.einsum(
        "kc,ctrl->trkl", select, masked, preferred_element_type=jnp.float32
    ).astype(jnp.bfloat16)
    routed = routed.reshape(all_frames, rows, n_sample, sends, lanes).transpose(2, 0, 1, 3, 4)
    outgoing = jnp.broadcast_to(
        routed[:, None], (n_sample, n_band, all_frames, rows, sends, lanes)
    ).reshape(n_sample * n_band, all_frames, rows, sends, lanes)
    units = w_gate.shape[1] // n_sample

    def of_units(weight, index, axis):
        return lax.dynamic_slice_in_dim(weight, index * units, units, axis=axis)

    others = [(group + d) % n_sample for d in range(1, n_sample)]
    outbound = [
        jnp.concatenate([of_units(w_gate.T, i, 0), of_units(w_up.T, i, 0)], axis=0) for i in others
    ]
    outgoing, outbound = lax.optimization_barrier((outgoing, outbound))
    got = lax.all_to_all(outgoing, ("sample", "band"), 0, 0, tiled=True)
    got = got.reshape(n_sample, n_band, all_frames, rows, sends, lanes)
    got = got.transpose(2, 1, 3, 0, 4, 5).reshape(all_frames, n_band * rows, clips, lanes)
    got = jnp.pad(got, ((0, 0), (2, 2), (0, 0), (0, 0)))
    cells = lax.dynamic_slice_in_dim(got, band * rows, rows + 4, axis=1)

    own_v = jnp.sum(
        w_down.astype(jnp.float32)
        * lax.dynamic_slice_in_dim(w_score, group * w_down.shape[1], w_down.shape[1])[None, :],
        axis=-1,
    )
    depth = w_gate.shape[0]
    arrived, v_parts = [], []
    for d in range(1, n_sample):
        route = [(i, (i + d) % n_sample) for i in range(n_sample)]
        arrived.append(lax.ppermute(outbound[d - 1], "sample", route))
        v_parts.append(lax.ppermute(of_units(own_v, others[d - 1], 0), "sample", route))

    slot_is = dest_slot[None, :] == jnp.arange(all_clips, dtype=jnp.int32)[:, None]
    len_slot = jnp.sum(jnp.where(slot_is, lengths[None, :], 0), axis=1)
    my_slots = lax.dynamic_slice_in_dim(len_slot, group * clips, clips)
    scalars = jnp.concatenate(
        [
            jnp.stack([band == 0, band == n_band - 1, stretch == 0]).astype(jnp.int32),
            frame0[None].astype(jnp.int32),
            my_slots,
        ]
    )
    decoded, band_sum = decode(
        scalars, cells, w_in, b_in, gain_mid, w_mid, b_mid, frames, rows, widths
    )
    decoded_out = decoded.transpose(2, 0, 1, 3)

    band_sum, v_parts = lax.optimization_barrier((band_sum, v_parts))
    band_sum = band_sum.reshape(n_band, frames * clips // n_band, chans)
    parts = lax.all_to_all(band_sum, "band", 0, 0, tiled=True)
    pooled = jnp.sum(parts, axis=0) / (rows * n_band * widths)
    pooled, arrived = lax.optimization_barrier((pooled, arrived))
    gate_parts = [of_units(w_gate, group, 1)] + [w[:units].T for w in arrived]
    up_parts = [of_units(w_up, group, 1)] + [w[units:].T for w in arrived]
    v_unit = of_units(own_v, group, 0) + sum(v_parts)
    pooled = spread(pooled.astype(jnp.bfloat16), ALL).reshape(-1, chans)
    tokens = jnp.dot(pooled, w_proj, preferred_element_type=jnp.float32).astype(jnp.bfloat16)
    token_f = tokens.astype(jnp.float32)
    normed = (
        token_f * lax.rsqrt(jnp.mean(token_f * token_f, axis=-1, keepdims=True) + 1e-06) * gain_tok
    ).astype(jnp.bfloat16)

    def product(parts):
        total = None
        for d in range(n_sample):
            source = (group - d) % n_sample
            rows_here = lax.dynamic_slice_in_dim(normed, source * depth, depth, axis=1)
            term = jnp.dot(rows_here, parts[d], preferred_element_type=jnp.float32)
            total = term if total is None else total + term
        return total

    hidden = (jax.nn.silu(product(gate_parts)) * product(up_parts)).astype(jnp.bfloat16)
    branch = jnp.sum(hidden.astype(jnp.float32) * v_unit[None, :], axis=-1)
    at_home = jnp.sum(token_f * w_score, axis=-1)
    first_device = (group == 0) & (stretch == 0) & (band == 0)
    partial = branch + jnp.where(first_device, at_home, 0.0)
    partial = partial.reshape(n_sample, n_stretch * frames, clips)
    lens_all = len_slot.reshape(n_sample, 1, clips)
    counted = jnp.arange(n_stretch * frames, dtype=jnp.int32)[None, :, None] < lens_all
    slot_part = jnp.sum(jnp.where(counted, partial, 0.0), axis=1).reshape(-1)
    slot_part = slot_part / len_slot.astype(jnp.float32)
    clip_part = jnp.sum(jnp.where(slot_is, slot_part[:, None], 0.0), axis=0)
    scores = jnp.sum(spread(clip_part, ALL), axis=0)
    return (decoded_out, scores)


def solution(mesh):
    in_specs = (
        P("sample", "stretch", "band", None),
        P(),
        P(),
        P(),
        P(),
        P(),
        P(),
        P(),
        P(),
        P(),
        P("sample", ("stretch", "band")),
        P("sample", ("stretch", "band")),
        P(("stretch", "band"), "sample"),
        P(),
    )
    out_specs = (P("sample", "stretch", "band", None), P())
    return jax.shard_map(body, mesh=mesh, in_specs=in_specs, out_specs=out_specs, check_vma=False)
```
